32 devices in a mesh: dom: 16 (over z, y, core), head: 2 (over x).
Axes of the slice: x: 2, y: 2, z: 4, core: 2. Of those that a mesh axis runs over, the one named last changes fastest.
Arguments:
- node_feats: bfloat16 [6144, 512], P('dom', 'head'), may hold values from -16 to 16
- tile_vals: bfloat16 [48, 4, 128, 128], P('dom'), may hold values from -0.375 to 0.375
- tile_counts: int32 [48], P('dom'), may hold values from 1 to 4
- tile_cols: int32 [48, 4], P('dom'), may hold values from 0 to 6
- send_rows: int32 [16, 4, 128], P('dom'), may hold values from 0 to 383, as said below
- w_msg: bfloat16 [512, 512], P(None, 'head'), may hold values from -0.25 to 0.25
- w_qkv: bfloat16 [3, 512, 512], P(None, None, 'head'), may hold values from -0.25 to 0.25
- w_out: bfloat16 [512, 512], P('head'), may hold values from -0.25 to 0.25
Outputs:
- updated: bfloat16 [6144, 512], P('dom', 'head')
The draws below stay inside these ranges and needn't reach their ends.
Inputs may be any that keep to these rules, and one draw needn't show every extreme that they name: `send_rows`: local row indices within the sending partition. `tile_cols`: block c < 3 of a partition's row table is its own row block c; block 3 + j is the block of 128 rows received with offset index j.
All inputs are finite; a program needn't handle non-finite values.
Results may differ from the reference program's by a relative error of at most 0.012.
The reference program's roundings to bfloat16 on the way count: a program that leaves them out, or rounds other values in their place, can miss the bound.
Values may be sent and summed in bfloat16 or wider, within the bound.
A program may use at most 64 MiB of HBM per device.

```python
import math
import jax
import jax.numpy as jnp
from jax import lax

D = 512
H = 8
DH = 64
BLK = 128
NODE_DEV = 384
BND = 128
REACH = 2
TPR = 4
RB = 3
EXT_BLK = 7
NODES = 6144
NB = 48
N_DOM = 16


def draw_node_feats(key, part):
    keys_all = jax.random.split(jax.random.fold_in(key, 11), 8)
    part_means = jax.random.normal(keys_all[6], (N_DOM, 1, D), jnp.float32)
    part_scales = jnp.exp(jax.random.uniform(keys_all[7], (N_DOM, 1, 1), jnp.float32, jnp.log(0.5), jnp.log(1.8)))
    noise = jnp.clip(jax.random.normal(keys_all[0], (NODES, D), jnp.float32), -6.0, 6.0) * 0.7
    base = ((noise.reshape(N_DOM, NODE_DEV, D) + part_means) * part_scales).reshape(NODES, D)
    base = jnp.clip(base, -16.0, 16.0)
    return base.astype(jnp.bfloat16)


def draw_send_rows(key, part):
    keys_all = jax.random.split(jax.random.fold_in(key, 23), 3)
    total = N_DOM * 2 * REACH * BND
    flat = jax.random.randint(keys_all[0], (total,), 0, NODE_DEV)
    lower_at = jax.random.randint(keys_all[1], (), 0, total // 2)
    upper_at = jax.random.randint(keys_all[2], (), total // 2, total)
    flat = flat.at[lower_at].set(0).at[upper_at].set(NODE_DEV - 1)
    return flat.reshape(N_DOM, 2 * REACH, BND).astype(jnp.int32)


def with_ends(entries, rng, smallest, largest):
    longest = entries.shape.index(max(entries.shape))
    spots = []
    for shift in (0, 1):
        where = [jax.random.randint(jax.random.fold_in(rng, axis), (), 0, length) for axis, length in enumerate(entries.shape)]
        where[longest] = (where[longest] + shift) % entries.shape[longest]
        spots.append(tuple(where))
    return entries.at[spots[0]].set(smallest).at[spots[1]].set(largest)


def steps_of(stream_key, shape, shards, low, high):
    def one(dim, blocks):
        heights = jax.random.uniform(jax.random.fold_in(jax.random.fold_in(stream_key, 6), dim), (blocks,), jnp.float32, low / len(shards), high / len(shards))
        return jnp.repeat(jnp.exp(heights), shape[dim] // blocks).reshape((-1,) + (1,) * (len(shape) - dim - 1))

    factor_of = one(*shards[0])
    for cut in shards[1:]:
        factor_of = factor_of * one(*cut)
    return factor_of


def bell_draw(key, extent, spread, bound, shards=(), kind=jnp.bfloat16):
    array = jax.random.normal(key, extent, jnp.float32) * spread
    if len(shards) > 0:
        array = steps_of(key, extent, shards, -0.22, 0.18) * array
    return jnp.clip(array, min=-bound, max=bound).astype(kind)


def setup_inputs(seed: int = 0) -> dict:
    seeds = jax.random.split(jax.random.key(seed), 9)
    node_feats = draw_node_feats(jax.random.fold_in(seeds[8], 71), 0)
    tile_vals = bell_draw(seeds[1], (NB, TPR, BLK, BLK), (2 * BLK) ** -0.5, 0.375, ((0, 16),))
    tile_counts = with_ends(jax.random.randint(seeds[2], (NB,), 1, TPR + 1), jax.random.fold_in(seeds[2], 1), 1, TPR).astype(jnp.int32)
    tile_cols = with_ends(jax.random.randint(seeds[3], (NB, TPR), 0, EXT_BLK), jax.random.fold_in(seeds[3], 1), 0, EXT_BLK - 1).astype(jnp.int32)
    send_rows = draw_send_rows(jax.random.fold_in(seeds[8], 71), 0)
    w_msg = bell_draw(seeds[5], (D, D), D ** -0.5, 0.25, ((1, 2),))
    w_qkv = bell_draw(seeds[6], (3, D, D), D ** -0.5, 0.25, ((2, 2),))
    w_out = bell_draw(seeds[7], (D, D), D ** -0.5, 0.25, ((0, 2),))
    return {"node_feats": node_feats, "tile_vals": tile_vals, "tile_counts": tile_counts, "tile_cols": tile_cols, "send_rows": send_rows, "w_msg": w_msg, "w_qkv": w_qkv, "w_out": w_out}


def offsets(reach_count):
    return [position - reach_count if position < reach_count else position - reach_count + 1 for position in range(2 * reach_count)]

def reference(node_feats, tile_vals, tile_counts, tile_cols, send_rows, w_msg, w_qkv, w_out):
    partitions = node_feats.reshape(N_DOM, NODE_DEV, D)
    owners = jnp.arange(N_DOM, dtype=jnp.int32)
    pieces = [partitions]
    for direction, shift_by in enumerate(offsets(REACH)):
        source = ((owners - shift_by) % N_DOM).astype(jnp.int32)
        chosen = partitions[source[:, None], send_rows[source, direction]]
        pieces.append(chosen)
    tables = jnp.concatenate(pieces, axis=1).reshape(N_DOM, EXT_BLK, BLK, D)
    tiles = tile_vals.reshape(N_DOM, RB, TPR, BLK, BLK)
    counts = tile_counts.reshape(N_DOM, RB)
    columns = tile_cols.reshape(N_DOM, RB, TPR)

    def one_part(operands):
        blocks, part_tiles, part_counts, part_cols = operands
        picked = blocks[part_cols].astype(jnp.float32)
        slots = jnp.arange(TPR, dtype=jnp.int32)
        live = slots[None, :] < part_counts[:, None]
        masked = jnp.where(live[:, :, None, None], part_tiles.astype(jnp.float32), jnp.zeros_like(part_tiles, dtype=jnp.float32))
        return jnp.einsum('rtij,rtjc->ric', masked, picked).reshape(NODE_DEV, D)
    aggregated = lax.map(one_part, (tables, tiles, counts, columns)).reshape(NODES, D).astype(jnp.bfloat16)
    message = jnp.maximum(jnp.dot(aggregated, w_msg, preferred_element_type=jnp.float32), 0.0)
    query = jnp.dot(node_feats, w_qkv[0], preferred_element_type=jnp.float32).astype(jnp.bfloat16)
    keys = jnp.dot(node_feats, w_qkv[1], preferred_element_type=jnp.float32).astype(jnp.bfloat16)
    values = jnp.dot(node_feats, w_qkv[2], preferred_element_type=jnp.float32).astype(jnp.bfloat16)
    scale = 1.0 / math.sqrt(DH)
    query_block = math.gcd(NODES, 1024)

    def one_head(operands):
        head_q, head_k, head_v = operands

        def one_block(block_q):
            scores = jnp.dot(block_q, head_k.T, preferred_element_type=jnp.float32) * scale
            weights = jnp.exp(scores - scores.max(axis=1, keepdims=True)).astype(jnp.bfloat16)
            total = weights.astype(jnp.float32).sum(axis=1, keepdims=True)
            return (jnp.dot(weights, head_v, preferred_element_type=jnp.float32) / total).astype(jnp.bfloat16)
        return lax.map(one_block, head_q.reshape(NODES // query_block, query_block, DH)).reshape(NODES, DH)
    split_q = query.reshape(NODES, H, DH).transpose(1, 0, 2)
    split_k = keys.reshape(NODES, H, DH).transpose(1, 0, 2)
    split_v = values.reshape(NODES, H, DH).transpose(1, 0, 2)
    heads_out = lax.map(one_head, (split_q, split_k, split_v)).transpose(1, 0, 2).reshape(NODES, D)
    attended = jnp.dot(heads_out, w_out, preferred_element_type=jnp.float32)
    return (node_feats.astype(jnp.float32) + message + attended).astype(jnp.bfloat16)
```

```python
import functools
import math

import jax
import jax.numpy as jnp
from jax import lax
from jax.experimental import pallas as pl
from jax.experimental.pallas import tpu as pltpu
from jax.sharding import PartitionSpec as P

DEPTH = 64
LANES = 128
MESH = pl.DeviceIdType.MESH
F32 = jnp.float32
BF16 = jnp.bfloat16


def offsets(count):
    reach = count // 2
    return [j - reach if j < reach else j - reach + 1 for j in range(count)]


def ring_next(chip, chips, step):
    depth = 4 if chips % 4 == 0 else 2
    width = chips // depth
    z, y = chip // width, chip % width
    if width == 1:
        return (chip + step + chips) % chips
    k = depth - 1 - z
    inner = width - 1
    odd = k % 2
    along = (1 - odd) * (y - 1) + odd * (width - 1 - y)
    first = 1 - jnp.minimum(y, 1)
    at = first * z + (1 - first) * (depth + k * inner + along)
    at = (at + step + chips) % chips
    far = 1 - jnp.minimum(jnp.maximum(at - (depth - 1), 0), 1)
    rest = jnp.maximum(at - depth, 0)
    k2 = rest // inner
    a2 = rest % inner
    odd2 = k2 % 2
    y2 = (1 - odd2) * (a2 + 1) + odd2 * (width - 1 - a2)
    z2 = depth - 1 - k2
    return far * (at * width) + (1 - far) * (z2 * width + y2)


def body(
    ndom, nhead, scale,
    live_ref, x_ref, tiles_ref, rows_ref, wmsg_ref, wqkv_ref, wout_ref,
    out_ref,
    table, chosen, wsend, wo, kv, qs, mx, acc, hg, msg,
    x_send, x_recv, w_send, w_recv, b_send, b_recv,
    r_send, r_recv, s_send, s_recv, h_send, h_recv,
):
    rows, cols = x_ref.shape
    width = qs.shape[2] * (kv.shape[3] // (2 * LANES))
    heads = qs.shape[0]
    half = rows // 2
    chips = ndom // 2
    steps = chips // 2
    blk = tiles_ref.shape[2]
    row_blocks, slots = tiles_ref.shape[0], tiles_ref.shape[1]
    reach = rows_ref.shape[0]
    blocks = row_blocks + reach
    me = lax.axis_index("dom")
    hd = lax.axis_index("head")
    chip, core = me // 2, me % 2
    right = (ring_next(chip, chips, 1) * 2 + core, hd)
    left = (ring_next(chip, chips, -1) * 2 + core, hd)
    sib = (chip * 2 + 1 - core, hd)
    near = [((me + o + ndom) % ndom, hd) for o in offsets(reach)]
    peers = [(me, (hd + k) % nhead) for k in range(1, nhead)]

    barrier = pltpu.get_barrier_semaphore()
    everyone = [right, left, sib] + near + peers
    for d in everyone:
        pl.semaphore_signal(barrier, inc=1, device_id=d, device_id_type=MESH)

    for k in range(nhead):
        wsend[k] = wout_ref[:, k * cols:(k + 1) * cols]
    table[hd, pl.ds(0, rows), :] = x_ref[...]
    pl.semaphore_wait(barrier, len(everyone))

    def copy(src, dst, ss, rs, to):
        return pltpu.make_async_remote_copy(
            src_ref=src, dst_ref=dst, send_sem=ss, recv_sem=rs, device_id=to, device_id_type=MESH
        )

    def x_copy(k):
        return copy(x_ref, table.at[hd, pl.ds(0, rows)], x_send.at[k], x_recv.at[k], peers[k])

    def w_copy(k):
        to = (hd + k + 1) % nhead
        return copy(wsend.at[to], wo.at[hd], w_send.at[k], w_recv.at[k], peers[k])

    def h_copy(k):
        return copy(hg.at[hd], hg.at[hd], h_send.at[k], h_recv.at[k], peers[k])

    def b_copy(j):
        dst = table.at[:, pl.ds(rows + j * blk, blk)]
        return copy(chosen.at[j], dst, b_send.at[j], b_recv.at[j], near[j])

    def part(ch):
        return pl.ds(ch * half, half)

    def ring_copy(s, way, ch):
        to = right if way == 0 else left
        if isinstance(s, int) and s == 1:
            src = kv.at[0, 0, part(ch)]
        else:
            src = kv.at[2 * s - 2, way, part(ch)]
        if isinstance(s, int) and s == steps:
            dst = kv.at[1, 0, part(ch)]
        else:
            dst = kv.at[2 * s, way, part(ch)]
        return copy(src, dst, r_send.at[s, way, ch], r_recv.at[s, way, ch], to)

    def sib_copy(s, way, ch):
        if isinstance(s, int) and s == 0:
            src, dst = kv.at[0, 0, part(ch)], kv.at[0, 1, part(ch)]
        elif isinstance(s, int) and s == steps:
            src, dst = kv.at[1, 0, part(ch)], kv.at[1, 1, part(ch)]
        else:
            src, dst = kv.at[2 * s, way, part(ch)], kv.at[2 * s + 1, way, part(ch)]
        return copy(src, dst, s_send.at[s, way, ch], s_recv.at[s, way, ch], sib)

    for k in range(nhead - 1):
        x_copy(k).start()

    def project(which, k, rs):
        w = wqkv_ref[which, pl.ds(pl.multiple_of(k * cols, cols), cols), :]
        x = table[k, rs, :]
        return jnp.dot(x, w, preferred_element_type=F32)

    def tiled(value, h):
        t = h // 2
        return value[:, t * LANES:(t + 1) * LANES]

    wo[hd] = wsend[hd]
    for h in range(heads):
        mx[h] = jnp.full((rows, LANES), -1e30, F32)
        acc[h] = jnp.zeros((rows, LANES), F32)

    whole = pl.ds(0, rows)
    begun = [project(i, hd, whole) for i in (1, 2)]
    for k in range(nhead - 1):
        x_copy(k).wait_recv()
        w_copy(k).start()
    for k in range(1, nhead):
        other = (hd + k) % nhead
        begun = [b + project(i, other, whole) for b, i in zip(begun, (1, 2))]
    for ch in range(2):
        for i in range(2):
            kv[0, 0, part(ch), i * width:(i + 1) * width] = begun[i][ch * half:(ch + 1) * half].astype(BF16)
        for way in range(2):
            ring_copy(1, way, ch).start()
        sib_copy(0, 0, ch).start()

    lane = lax.broadcasted_iota(jnp.int32, (1, LANES), 1)

    def mine(h):
        return (lane // DEPTH) == (h % 2)

    query = project(0, hd, whole)
    for k in range(1, nhead):
        query = query + project(0, (hd + k) % nhead, whole)
    query = query.astype(BF16)
    for h in range(heads):
        tile = tiled(query, h)
        qs[h] = jnp.where(mine(h), tile, jnp.zeros_like(tile))

    line = lax.broadcasted_iota(jnp.int32, (rows, blk), 0)
    for j in range(reach):
        pick = jnp.where(line == rows_ref[j:j + 1, :], 1.0, 0.0).astype(BF16)
        for k in range(nhead):
            got = lax.dot_general(
                pick, table[k, pl.ds(0, rows), :], (((0,), (0,)), ((), ())), preferred_element_type=F32
            )
            chosen[j, k] = got.astype(BF16)
        b_copy(j).start()

    factor = scale * math.log2(math.e)

    def attend(at):
        for h in range(heads):
            t = h // 2
            keys = kv[at, :, :, t * LANES:(t + 1) * LANES].reshape(2 * rows, LANES)
            values = kv[at, :, :, width + t * LANES:width + (t + 1) * LANES].reshape(2 * rows, LANES)
            values = jnp.where(mine(h), values, jnp.ones_like(values))
            s = lax.dot_general(qs[h], keys, (((1,), (1,)), ((), ())), preferred_element_type=F32)
            old = mx[h]
            new = jnp.maximum(old, jnp.max(s, axis=1, keepdims=True))
            p = jnp.exp2((s - new[:, :1]) * factor).astype(BF16)
            acc[h] = acc[h] * jnp.exp2((old - new) * factor) + jnp.dot(
                p, values, preferred_element_type=F32
            )
            mx[h] = new

    for ch in range(2):
        sib_copy(0, 0, ch).wait_recv()
    attend(0)

    def arrive(s, last):
        for ch in range(2):
            for way in range(2):
                ring_copy(s, way, ch).wait_recv()
                if not last or way == ch:
                    ring_copy_next(s, way, ch, last).start()
                sib_copy(s, way, ch).start()

    def ring_copy_next(s, way, ch, last):
        if last:
            return ring_copy(steps, way, ch)
        return ring_copy(s + 1, way, ch)

    def taken(s):
        for ch in range(2):
            for way in range(2):
                sib_copy(s, way, ch).wait_recv()

    def turn(i, carry):
        s = i + 1
        arrive(s, False)
        attend(2 * s)
        taken(s)
        attend(2 * s + 1)
        return carry

    lax.fori_loop(0, steps - 2, turn, 0)

    s = steps - 1
    arrive(s, True)
    for j in range(reach):
        b_copy(j).wait_recv()
    for r in range(row_blocks):
        total = [jnp.zeros((blk, cols), F32) for _ in range(nhead)]
        for t in range(slots):
            tile = tiles_ref[r, t]
            place = live_ref[r * slots + t:r * slots + t + 1, :]
            spread = jnp.concatenate(
                [tile * jnp.where(place == b, 1.0, 0.0).astype(BF16) for b in range(blocks)], axis=1
            )
            for k in range(nhead):
                total[k] = total[k] + jnp.dot(spread, table[k], preferred_element_type=F32)
        sent = jnp.zeros((blk, cols), F32)
        for k in range(nhead):
            sent = sent + jnp.dot(
                total[k].astype(BF16), wmsg_ref[k * cols:(k + 1) * cols, :], preferred_element_type=F32
            )
        msg[r * blk:(r + 1) * blk, :] = jnp.maximum(sent, 0.0) + x_ref[r * blk:(r + 1) * blk, :].astype(F32)
    attend(2 * s)
    for ch in range(2):
        ring_copy(steps, ch, ch).wait_recv()
        sib_copy(steps, 0, ch).start()
    taken(s)
    attend(2 * s + 1)
    for ch in range(2):
        sib_copy(steps, 0, ch).wait_recv()
    attend(1)

    for t in range((heads + 1) // 2):
        made = jnp.zeros((rows, LANES), F32)
        for h in range(2 * t, min(2 * t + 2, heads)):
            a = acc[h]
            made = jnp.where(mine(h), a / pltpu.roll(a, DEPTH, 1), made)
        hg[hd, :, t * LANES:(t + 1) * LANES] = made.astype(BF16)
    for k in range(nhead - 1):
        h_copy(k).start()
    result = msg[...] + jnp.dot(hg[hd], wo[hd], preferred_element_type=F32)
    for k in range(nhead - 1):
        w_copy(k).wait_recv()
        h_copy(k).wait_recv()
    for k in range(1, nhead):
        other = (hd + k) % nhead
        result = result + jnp.dot(hg[other], wo[other], preferred_element_type=F32)
    out_ref[...] = result.astype(BF16)

    for k in range(nhead - 1):
        x_copy(k).wait_send()
        w_copy(k).wait_send()
        h_copy(k).wait_send()
    for j in range(reach):
        b_copy(j).wait_send()
    for ch in range(2):
        sib_copy(0, 0, ch).wait_send()
        sib_copy(steps, 0, ch).wait_send()
        ring_copy(steps, ch, ch).wait_send()
        for way in range(2):
            ring_copy(1, way, ch).wait_send()

    def sent_all(i, carry):
        for ch in range(2):
            for way in range(2):
                sib_copy(i + 1, way, ch).wait_send()
        return carry

    def sent_ring(i, carry):
        for ch in range(2):
            for way in range(2):
                ring_copy(i + 2, way, ch).wait_send()
        return carry

    lax.fori_loop(0, steps - 1, sent_all, 0)
    lax.fori_loop(0, steps - 2, sent_ring, 0)


def local(ndom, nhead, node_feats, tile_vals, tile_counts, tile_cols, send_rows, w_msg, w_qkv, w_out):
    rows, cols = node_feats.shape
    blk = tile_vals.shape[2]
    reach = send_rows.shape[1]
    heads = cols // DEPTH
    width = -(-cols // LANES) * LANES
    if width != cols:
        w_qkv = jnp.pad(w_qkv, ((0, 0), (0, 0), (0, width - cols)))
        w_out = jnp.pad(w_out, ((0, width - cols), (0, 0)))
    steps = ndom // 4
    dma = pltpu.SemaphoreType.DMA
    others = max(nhead - 1, 1)
    vmem = pl.BlockSpec(memory_space=pltpu.VMEM)
    slot = lax.broadcasted_iota(jnp.int32, tile_cols.shape, 1)
    live = jnp.where(slot < tile_counts[:, None], tile_cols, -1).reshape(-1, 1)
    live = jnp.broadcast_to(live, (live.shape[0], blk))
    return pl.pallas_call(
        functools.partial(body, ndom, nhead, 1.0 / math.sqrt(DEPTH)),
        out_shape=jax.ShapeDtypeStruct((rows, cols), BF16),
        in_specs=[vmem] * 7,
        out_specs=vmem,
        scratch_shapes=[
            pltpu.VMEM((nhead, rows + reach * blk, cols), BF16),
            pltpu.VMEM((reach, nhead, blk, cols), BF16),
            pltpu.VMEM((nhead, width, cols), BF16),
            pltpu.VMEM((nhead, width, cols), BF16),
            pltpu.VMEM((2 * steps, 2, rows, 2 * width), BF16),
            pltpu.VMEM((heads, rows, LANES), BF16),
            pltpu.VMEM((heads, rows, LANES), F32),
            pltpu.VMEM((heads, rows, LANES), F32),
            pltpu.VMEM((nhead, rows, width), BF16),
            pltpu.VMEM((rows, cols), F32),
            dma((others,)), dma((others,)),
            dma((others,)), dma((others,)),
            dma((reach,)), dma((reach,)),
            dma((steps + 1, 2, 2)), dma((steps + 1, 2, 2)),
            dma((steps + 1, 2, 2)), dma((steps + 1, 2, 2)),
            dma((others,)), dma((others,)),
        ],
        compiler_params=pltpu.CompilerParams(
            collective_id=0, has_side_effects=True, vmem_limit_bytes=48 * 1024 * 1024
        ),
    )(live, node_feats, tile_vals, send_rows[0], w_msg, w_qkv, w_out)


def solution(mesh):
    placed = (
        P("dom", "head"),
        P("dom", None, None, None),
        P("dom"),
        P("dom", None),
        P("dom", None, None),
        P(None, "head"),
        P(None, None, "head"),
        P("head", None),
    )
    return jax.shard_map(
        functools.partial(local, mesh.shape["dom"], mesh.shape["head"]),
        mesh=mesh, in_specs=placed, out_specs=P("dom", "head"), check_vma=False,
    )
```

```python
import functools
import math

import jax
import jax.numpy as jnp
from jax import lax
from jax.experimental import pallas as pl
from jax.experimental.pallas import tpu as pltpu
from jax.sharding import PartitionSpec as P

DEPTH = 64
LANES = 128
MESH = pl.DeviceIdType.MESH
F32 = jnp.float32
BF16 = jnp.bfloat16


def offsets(count):
    reach = count // 2
    return [j - reach if j < reach else j - reach + 1 for j in range(count)]


def ring_next(chip, chips, step):
    depth = 4 if chips % 4 == 0 else 2
    width = chips // depth
    z, y = chip // width, chip % width
    if width == 1:
        return (chip + step + chips) % chips
    k = depth - 1 - z
    inner = width - 1
    odd = k % 2
    along = (1 - odd) * (y - 1) + odd * (width - 1 - y)
    first = 1 - jnp.minimum(y, 1)
    at = first * z + (1 - first) * (depth + k * inner + along)
    at = (at + step + chips) % chips
    far = 1 - jnp.minimum(jnp.maximum(at - (depth - 1), 0), 1)
    rest = jnp.maximum(at - depth, 0)
    k2 = rest // inner
    a2 = rest % inner
    odd2 = k2 % 2
    y2 = (1 - odd2) * (a2 + 1) + odd2 * (width - 1 - a2)
    z2 = depth - 1 - k2
    return far * (at * width) + (1 - far) * (z2 * width + y2)


def body(
    ndom, nhead, scale,
    live_in, x_ref, tiles_in, rows_in, wmsg_in, wqkv_in, wout_in,
    out_ref,
    live_ref, tiles_ref, rows_ref, wmsg_ref, wqkv_ref, wout_ref, in_sem,
    table, chosen, wsend, wo, kv, qs, mx, acc, hg, msg,
    x_send, x_recv, w_send, w_recv, b_send, b_recv, c_send, c_recv,
    r_send, r_recv, s_send, s_recv, h_send, h_recv,
):
    rows, cols = x_ref.shape
    width = qs.shape[2] * (kv.shape[3] // (2 * LANES))
    heads = qs.shape[0]
    half = rows // 2
    chips = ndom // 2
    steps = chips // 2
    blk = tiles_ref.shape[2]
    row_blocks, slots = tiles_ref.shape[0], tiles_ref.shape[1]
    reach = rows_ref.shape[0]
    blocks = row_blocks + reach
    me = lax.axis_index("dom")
    hd = lax.axis_index("head")
    chip, core = me // 2, me % 2
    right = (ring_next(chip, chips, 1) * 2 + core, hd)
    left = (ring_next(chip, chips, -1) * 2 + core, hd)
    sib = (chip * 2 + 1 - core, hd)
    near = [((me + o + ndom) % ndom, hd) for o in offsets(reach)]
    peers = [(me, (hd + k) % nhead) for k in range(1, nhead)]

    barrier = pltpu.get_barrier_semaphore()
    everyone = [right, left, sib] + near + peers
    for d in everyone:
        pl.semaphore_signal(barrier, inc=1, device_id=d, device_id_type=MESH)

    def fetch(i, src, dst):
        return pltpu.make_async_copy(src, dst, in_sem.at[i])

    get_x = fetch(0, x_ref, table.at[hd, pl.ds(0, rows)])
    get_qkv = fetch(1, wqkv_in, wqkv_ref)
    get_rows = fetch(2, rows_in, rows_ref)
    get_out = fetch(3, wout_in, wout_ref)
    get_live = fetch(4, live_in, live_ref)
    get_msg = fetch(5, wmsg_in, wmsg_ref)
    get_tiles = fetch(6, tiles_in, tiles_ref)
    for get in (get_x, get_qkv, get_rows, get_out, get_live, get_msg, get_tiles):
        get.start()
    pl.semaphore_wait(barrier, len(everyone))

    def copy(src, dst, ss, rs, to):
        return pltpu.make_async_remote_copy(
            src_ref=src, dst_ref=dst, send_sem=ss, recv_sem=rs, device_id=to, device_id_type=MESH
        )

    def x_copy(k):
        return copy(x_ref, table.at[hd, pl.ds(0, rows)], x_send.at[k], x_recv.at[k], peers[k])

    def w_copy(k):
        to = (hd + k + 1) % nhead
        return copy(wsend.at[to], wo.at[hd], w_send.at[k], w_recv.at[k], peers[k])

    def h_copy(k):
        return copy(hg.at[hd], hg.at[hd], h_send.at[k], h_recv.at[k], peers[k])

    def b_copy(j):
        dst = table.at[hd, pl.ds(rows + j * blk, blk)]
        return copy(chosen.at[j], dst, b_send.at[j], b_recv.at[j], near[j])

    def c_copy(j, k):
        both = table.at[hd, pl.ds(rows + j * blk, blk)]
        return copy(both, both, c_send.at[j, k], c_recv.at[j, k], peers[k])

    def part(ch):
        return pl.ds(ch * half, half)

    def ring_copy(s, way, ch):
        to = right if way == 0 else left
        if isinstance(s, int) and s == 1:
            src = kv.at[0, 0, part(ch)]
        else:
            src = kv.at[2 * s - 2, way, part(ch)]
        if isinstance(s, int) and s == steps:
            dst = kv.at[1, 0, part(ch)]
        else:
            dst = kv.at[2 * s, way, part(ch)]
        return copy(src, dst, r_send.at[s, way, ch], r_recv.at[s, way, ch], to)

    def sib_copy(s, way, ch):
        if isinstance(s, int) and s == 0:
            src, dst = kv.at[0, 0, part(ch)], kv.at[0, 1, part(ch)]
        elif isinstance(s, int) and s == steps:
            src, dst = kv.at[1, 0, part(ch)], kv.at[1, 1, part(ch)]
        else:
            src, dst = kv.at[2 * s, way, part(ch)], kv.at[2 * s + 1, way, part(ch)]
        return copy(src, dst, s_send.at[s, way, ch], s_recv.at[s, way, ch], sib)

    for k in range(nhead - 1):
        x_copy(k).start()

    def project(which, k, rs):
        w = wqkv_ref[which, pl.ds(pl.multiple_of(k * cols, cols), cols), :]
        x = table[k, rs, :]
        return jnp.dot(x, w, preferred_element_type=F32)

    def tiled(value, h):
        t = h // 2
        return value[:, t * LANES:(t + 1) * LANES]

    for h in range(heads):
        mx[h] = jnp.full((rows, LANES), -1e30, F32)
        acc[h] = jnp.zeros((rows, LANES), F32)

    get_x.wait()
    get_qkv.wait()
    whole = pl.ds(0, rows)
    begun = [project(i, hd, whole) for i in (1, 2)]
    for k in range(nhead - 1):
        x_copy(k).wait_recv()
    for k in range(1, nhead):
        other = (hd + k) % nhead
        begun = [b + project(i, other, whole) for b, i in zip(begun, (1, 2))]
    for ch in range(2):
        for i in range(2):
            kv[0, 0, part(ch), i * width:(i + 1) * width] = begun[i][ch * half:(ch + 1) * half].astype(BF16)
        for way in range(2):
            ring_copy(1, way, ch).start()
        sib_copy(0, 0, ch).start()

    lane = lax.broadcasted_iota(jnp.int32, (1, LANES), 1)

    def mine(h):
        return (lane // DEPTH) == (h % 2)

    query = project(0, hd, whole)
    for k in range(1, nhead):
        query = query + project(0, (hd + k) % nhead, whole)
    query = query.astype(BF16)
    for h in range(heads):
        tile = tiled(query, h)
        qs[h] = jnp.where(mine(h), tile, jnp.zeros_like(tile))

    get_rows.wait()
    line = lax.broadcasted_iota(jnp.int32, (rows, blk), 0)
    for j in range(reach):
        pick = jnp.where(line == rows_ref[j:j + 1, :], 1.0, 0.0).astype(BF16)
        got = lax.dot_general(
            pick, table[hd, pl.ds(0, rows), :], (((0,), (0,)), ((), ())), preferred_element_type=F32
        )
        chosen[j] = got.astype(BF16)
        b_copy(j).start()

    factor = scale * math.log2(math.e)

    def attend(at):
        for h in range(heads):
            t = h // 2
            keys = kv[at, :, :, t * LANES:(t + 1) * LANES].reshape(2 * rows, LANES)
            values = kv[at, :, :, width + t * LANES:width + (t + 1) * LANES].reshape(2 * rows, LANES)
            values = jnp.where(mine(h), values, jnp.ones_like(values))
            s = lax.dot_general(qs[h], keys, (((1,), (1,)), ((), ())), preferred_element_type=F32)
            old = mx[h]
            new = jnp.maximum(old, jnp.max(s, axis=1, keepdims=True))
            p = jnp.exp2((s - new[:, :1]) * factor).astype(BF16)
            acc[h] = acc[h] * jnp.exp2((old - new) * factor) + jnp.dot(
                p, values, preferred_element_type=F32
            )
            mx[h] = new

    get_out.wait()
    for k in range(nhead):
        wsend[k] = wout_ref[:, k * cols:(k + 1) * cols]
    wo[hd] = wsend[hd]
    for k in range(nhead - 1):
        w_copy(k).start()
    for ch in range(2):
        sib_copy(0, 0, ch).wait_recv()
    attend(0)

    def arrive(s, last):
        for ch in range(2):
            for way in range(2):
                ring_copy(s, way, ch).wait_recv()
                if not last or way == ch:
                    ring_copy_next(s, way, ch, last).start()
                sib_copy(s, way, ch).start()

    def ring_copy_next(s, way, ch, last):
        if last:
            return ring_copy(steps, way, ch)
        return ring_copy(s + 1, way, ch)

    def taken(s):
        for ch in range(2):
            for way in range(2):
                sib_copy(s, way, ch).wait_recv()

    def turn(i, carry):
        s = i + 1
        arrive(s, False)
        attend(2 * s)
        taken(s)
        attend(2 * s + 1)
        return carry

    lax.fori_loop(0, steps - 2, turn, 0)

    s = steps - 1
    arrive(s, True)
    for j in range(reach):
        b_copy(j).wait_recv()
        for k in range(nhead - 1):
            c_copy(j, k).start()
    attend(2 * s)
    get_live.wait()
    get_msg.wait()
    get_tiles.wait()
    for j in range(reach):
        for k in range(nhead - 1):
            c_copy(j, k).wait_recv()
    for r in range(row_blocks):
        total = [jnp.zeros((blk, cols), F32) for _ in range(nhead)]
        for t in range(slots):
            tile = tiles_ref[r, t]
            place = live_ref[r * slots + t:r * slots + t + 1, :]
            spread = jnp.concatenate(
                [tile * jnp.where(place == b, 1.0, 0.0).astype(BF16) for b in range(blocks)], axis=1
            )
            for k in range(nhead):
                total[k] = total[k] + jnp.dot(spread, table[k], preferred_element_type=F32)
        sent = jnp.zeros((blk, cols), F32)
        for k in range(nhead):
            sent = sent + jnp.dot(
                total[k].astype(BF16), wmsg_ref[k * cols:(k + 1) * cols, :], preferred_element_type=F32
            )
        msg[r * blk:(r + 1) * blk, :] = jnp.maximum(sent, 0.0) + table[hd, r * blk:(r + 1) * blk, :].astype(F32)
    for ch in range(2):
        ring_copy(steps, ch, ch).wait_recv()
        sib_copy(steps, 0, ch).start()
    taken(s)
    attend(2 * s + 1)
    for ch in range(2):
        sib_copy(steps, 0, ch).wait_recv()
    attend(1)

    for t in range((heads + 1) // 2):
        made = jnp.zeros((rows, LANES), F32)
        for h in range(2 * t, min(2 * t + 2, heads)):
            a = acc[h]
            made = jnp.where(mine(h), a / pltpu.roll(a, DEPTH, 1), made)
        hg[hd, :, t * LANES:(t + 1) * LANES] = made.astype(BF16)
    for k in range(nhead - 1):
        h_copy(k).start()
    result = msg[...] + jnp.dot(hg[hd], wo[hd], preferred_element_type=F32)
    for k in range(nhead - 1):
        w_copy(k).wait_recv()
        h_copy(k).wait_recv()
    for k in range(1, nhead):
        other = (hd + k) % nhead
        result = result + jnp.dot(hg[other], wo[other], preferred_element_type=F32)
    out_ref[...] = result.astype(BF16)

    for k in range(nhead - 1):
        x_copy(k).wait_send()
        w_copy(k).wait_send()
        h_copy(k).wait_send()
    for j in range(reach):
        b_copy(j).wait_send()
        for k in range(nhead - 1):
            c_copy(j, k).wait_send()
    for ch in range(2):
        sib_copy(0, 0, ch).wait_send()
        sib_copy(steps, 0, ch).wait_send()
        ring_copy(steps, ch, ch).wait_send()
        for way in range(2):
            ring_copy(1, way, ch).wait_send()

    def sent_all(i, carry):
        for ch in range(2):
            for way in range(2):
                sib_copy(i + 1, way, ch).wait_send()
        return carry

    def sent_ring(i, carry):
        for ch in range(2):
            for way in range(2):
                ring_copy(i + 2, way, ch).wait_send()
        return carry

    lax.fori_loop(0, steps - 1, sent_all, 0)
    lax.fori_loop(0, steps - 2, sent_ring, 0)


def local(ndom, nhead, node_feats, tile_vals, tile_counts, tile_cols, send_rows, w_msg, w_qkv, w_out):
    rows, cols = node_feats.shape
    blk = tile_vals.shape[2]
    reach = send_rows.shape[1]
    heads = cols // DEPTH
    width = -(-cols // LANES) * LANES
    if width != cols:
        w_qkv = jnp.pad(w_qkv, ((0, 0), (0, 0), (0, width - cols)))
        w_out = jnp.pad(w_out, ((0, width - cols), (0, 0)))
    steps = ndom // 4
    dma = pltpu.SemaphoreType.DMA
    others = max(nhead - 1, 1)
    vmem = pl.BlockSpec(memory_space=pltpu.VMEM)
    slot = lax.broadcasted_iota(jnp.int32, tile_cols.shape, 1)
    live = jnp.where(slot < tile_counts[:, None], tile_cols, -1).reshape(-1, 1)
    live = jnp.broadcast_to(live, (live.shape[0], blk))
    return pl.pallas_call(
        functools.partial(body, ndom, nhead, 1.0 / math.sqrt(DEPTH)),
        out_shape=jax.ShapeDtypeStruct((rows, cols), BF16),
        in_specs=[pl.BlockSpec(memory_space=pltpu.HBM)] * 7,
        out_specs=vmem,
        scratch_shapes=[
            pltpu.VMEM(live.shape, jnp.int32),
            pltpu.VMEM(tile_vals.shape, BF16),
            pltpu.VMEM(send_rows.shape[1:], jnp.int32),
            pltpu.VMEM(w_msg.shape, BF16),
            pltpu.VMEM(w_qkv.shape, BF16),
            pltpu.VMEM(w_out.shape, BF16),
            dma((7,)),
            pltpu.VMEM((nhead, rows + reach * blk, cols), BF16),
            pltpu.VMEM((reach, blk, cols), BF16),
            pltpu.VMEM((nhead, width, cols), BF16),
            pltpu.VMEM((nhead, width, cols), BF16),
            pltpu.VMEM((2 * steps, 2, rows, 2 * width), BF16),
            pltpu.VMEM((heads, rows, LANES), BF16),
            pltpu.VMEM((heads, rows, LANES), F32),
            pltpu.VMEM((heads, rows, LANES), F32),
            pltpu.VMEM((nhead, rows, width), BF16),
            pltpu.VMEM((rows, cols), F32),
            dma((others,)), dma((others,)),
            dma((others,)), dma((others,)),
            dma((reach,)), dma((reach,)),
            dma((reach, others)), dma((reach, others)),
            dma((steps + 1, 2, 2)), dma((steps + 1, 2, 2)),
            dma((steps + 1, 2, 2)), dma((steps + 1, 2, 2)),
            dma((others,)), dma((others,)),
        ],
        compiler_params=pltpu.CompilerParams(
            collective_id=0, has_side_effects=True, vmem_limit_bytes=63 * 1024 * 1024
        ),
    )(live, node_feats, tile_vals, send_rows[0], w_msg, w_qkv, w_out)


def solution(mesh):
    placed = (
        P("dom", "head"),
        P("dom", None, None, None),
        P("dom"),
        P("dom", None),
        P("dom", None, None),
        P(None, "head"),
        P(None, None, "head"),
        P("head", None),
    )
    return jax.shard_map(
        functools.partial(local, mesh.shape["dom"], mesh.shape["head"]),
        mesh=mesh, in_specs=placed, out_specs=P("dom", "head"), check_vma=False,
    )
```

```python
import functools
import math

import jax
import jax.numpy as jnp
from jax import lax
from jax.experimental import pallas as pl
from jax.experimental.pallas import tpu as pltpu
from jax.sharding import PartitionSpec as P

DEPTH = 64
LANES = 128
MESH = pl.DeviceIdType.MESH
F32 = jnp.float32
BF16 = jnp.bfloat16


def offsets(count):
    reach = count // 2
    return [j - reach if j < reach else j - reach + 1 for j in range(count)]


def ring_next(chip, chips, step):
    depth = 4 if chips % 4 == 0 else 2
    width = chips // depth
    z, y = chip // width, chip % width
    if width == 1:
        return (chip + step + chips) % chips
    k = depth - 1 - z
    inner = width - 1
    odd = k % 2
    along = (1 - odd) * (y - 1) + odd * (width - 1 - y)
    first = 1 - jnp.minimum(y, 1)
    at = first * z + (1 - first) * (depth + k * inner + along)
    at = (at + step + chips) % chips
    far = 1 - jnp.minimum(jnp.maximum(at - (depth - 1), 0), 1)
    rest = jnp.maximum(at - depth, 0)
    k2 = rest // inner
    a2 = rest % inner
    odd2 = k2 % 2
    y2 = (1 - odd2) * (a2 + 1) + odd2 * (width - 1 - a2)
    z2 = depth - 1 - k2
    return far * (at * width) + (1 - far) * (z2 * width + y2)


def body(
    ndom, nhead, scale,
    live_in, x_ref, tiles_in, rows_in, wmsg_in, wqkv_in, wout_in,
    out_ref,
    live_ref, tiles_ref, rows_ref, wmsg_ref, wqkv_ref, wout_ref, in_sem,
    table, chosen, wsend, wo, kv, qs, mx, acc, hg, msg,
    x_send, x_recv, w_send, w_recv, b_send, b_recv, c_send, c_recv,
    r_send, r_recv, s_send, s_recv, h_send, h_recv,
    f_send, f_recv, fx,
):
    rows, cols = x_ref.shape
    width = qs.shape[2] * (kv.shape[3] // (2 * LANES))
    heads = qs.shape[0]
    half = rows // 2
    chips = ndom // 2
    steps = chips // 2
    blk = tiles_ref.shape[2]
    row_blocks, slots = tiles_ref.shape[0], tiles_ref.shape[1]
    reach = rows_ref.shape[0]
    blocks = row_blocks + reach
    me = lax.axis_index("dom")
    hd = lax.axis_index("head")
    chip, core = me // 2, me % 2
    right = (ring_next(chip, chips, 1) * 2 + core, hd)
    left = (ring_next(chip, chips, -1) * 2 + core, hd)
    sib = (chip * 2 + 1 - core, hd)
    near = [((me + o + ndom) % ndom, hd) for o in offsets(reach)]
    peers = [(me, (hd + k) % nhead) for k in range(1, nhead)]

    barrier = pltpu.get_barrier_semaphore()
    everyone = [right, left, sib] + near + peers
    for d in everyone:
        pl.semaphore_signal(barrier, inc=1, device_id=d, device_id_type=MESH)

    def fetch(i, src, dst):
        return pltpu.make_async_copy(src, dst, in_sem.at[i])

    get_x = fetch(0, x_ref, table.at[hd, pl.ds(0, rows)])
    get_qkv = fetch(1, wqkv_in, wqkv_ref)
    get_rows = fetch(2, rows_in, rows_ref)
    get_out = fetch(3, wout_in, wout_ref)
    get_live = fetch(4, live_in, live_ref)
    get_msg = fetch(5, wmsg_in, wmsg_ref)
    get_tiles = fetch(6, tiles_in, tiles_ref)
    for get in (get_x, get_qkv, get_rows, get_out, get_live, get_msg, get_tiles):
        get.start()
    pl.semaphore_wait(barrier, len(everyone))

    def copy(src, dst, ss, rs, to):
        return pltpu.make_async_remote_copy(
            src_ref=src, dst_ref=dst, send_sem=ss, recv_sem=rs, device_id=to, device_id_type=MESH
        )

    def x_copy(k):
        return copy(x_ref, table.at[hd, pl.ds(0, rows)], x_send.at[k], x_recv.at[k], peers[k])

    def w_copy(k):
        to = (hd + k + 1) % nhead
        return copy(wsend.at[to], wo.at[hd], w_send.at[k], w_recv.at[k], peers[k])

    def h_copy(k):
        return copy(hg.at[hd], hg.at[hd], h_send.at[k], h_recv.at[k], peers[k])

    def b_copy(j):
        dst = table.at[hd, pl.ds(rows + j * blk, blk)]
        return copy(chosen.at[j], dst, b_send.at[j], b_recv.at[j], near[j])

    def c_copy(j, k):
        both = table.at[hd, pl.ds(rows + j * blk, blk)]
        return copy(both, both, c_send.at[j, k], c_recv.at[j, k], peers[k])

    def part(ch):
        return pl.ds(ch * half, half)

    def ring_copy(s, way, ch):
        to = right if way == 0 else left
        if ch == 1:
            src = x_ref.at[part(1)] if isinstance(s, int) and s == 1 else fx.at[s - 1, way, hd]
            return copy(src, fx.at[s, way, hd], r_send.at[s, way, ch], r_recv.at[s, way, ch], to)
        if isinstance(s, int) and s == 1:
            src = kv.at[0, 0, part(ch)]
        else:
            src = kv.at[2 * s - 2, way, part(ch)]
        if isinstance(s, int) and s == steps:
            dst = kv.at[1, 0, part(ch)]
        else:
            dst = kv.at[2 * s, way, part(ch)]
        return copy(src, dst, r_send.at[s, way, ch], r_recv.at[s, way, ch], to)

    def f_copy(s, way, k):
        both = fx.at[s, way, hd]
        return copy(both, both, f_send.at[s, way, k], f_recv.at[s, way, k], peers[k])

    def sib_copy(s, way, ch):
        if isinstance(s, int) and s == 0:
            src, dst = kv.at[0, 0, part(ch)], kv.at[0, 1, part(ch)]
        elif isinstance(s, int) and s == steps:
            src, dst = kv.at[1, 0, part(ch)], kv.at[1, 1, part(ch)]
        else:
            src, dst = kv.at[2 * s, way, part(ch)], kv.at[2 * s + 1, way, part(ch)]
        return copy(src, dst, s_send.at[s, way, ch], s_recv.at[s, way, ch], sib)

    for k in range(nhead - 1):
        x_copy(k).start()
    for way in range(2):
        ring_copy(1, way, 1).start()

    def project(which, k, rs):
        w = wqkv_ref[which, pl.ds(pl.multiple_of(k * cols, cols), cols), :]
        x = table[k, rs, :]
        return jnp.dot(x, w, preferred_element_type=F32)

    def tiled(value, h):
        t = h // 2
        return value[:, t * LANES:(t + 1) * LANES]

    for h in range(heads):
        mx[h] = jnp.full((rows, LANES), -1e30, F32)
        acc[h] = jnp.zeros((rows, LANES), F32)

    get_x.wait()
    get_qkv.wait()
    whole = pl.ds(0, rows)
    begun = [project(i, hd, whole) for i in (1, 2)]
    for k in range(nhead - 1):
        x_copy(k).wait_recv()
    for k in range(1, nhead):
        other = (hd + k) % nhead
        begun = [b + project(i, other, whole) for b, i in zip(begun, (1, 2))]
    for ch in range(2):
        for i in range(2):
            kv[0, 0, part(ch), i * width:(i + 1) * width] = begun[i][ch * half:(ch + 1) * half].astype(BF16)
        for way in range(2):
            if ch == 0:
                ring_copy(1, way, ch).start()
        sib_copy(0, 0, ch).start()

    lane = lax.broadcasted_iota(jnp.int32, (1, LANES), 1)

    def mine(h):
        return (lane // DEPTH) == (h % 2)

    query = project(0, hd, whole)
    for k in range(1, nhead):
        query = query + project(0, (hd + k) % nhead, whole)
    query = query.astype(BF16)
    for h in range(heads):
        tile = tiled(query, h)
        qs[h] = jnp.where(mine(h), tile, jnp.zeros_like(tile))

    get_rows.wait()
    line = lax.broadcasted_iota(jnp.int32, (rows, blk), 0)
    for j in range(reach):
        pick = jnp.where(line == rows_ref[j:j + 1, :], 1.0, 0.0).astype(BF16)
        got = lax.dot_general(
            pick, table[hd, pl.ds(0, rows), :], (((0,), (0,)), ((), ())), preferred_element_type=F32
        )
        chosen[j] = got.astype(BF16)
        b_copy(j).start()

    factor = scale * math.log2(math.e)

    def attend(at):
        for h in range(heads):
            t = h // 2
            keys = kv[at, :, :, t * LANES:(t + 1) * LANES].reshape(2 * rows, LANES)
            values = kv[at, :, :, width + t * LANES:width + (t + 1) * LANES].reshape(2 * rows, LANES)
            values = jnp.where(mine(h), values, jnp.ones_like(values))
            s = lax.dot_general(qs[h], keys, (((1,), (1,)), ((), ())), preferred_element_type=F32)
            old = mx[h]
            new = jnp.maximum(old, jnp.max(s, axis=1, keepdims=True))
            p = jnp.exp2((s - new[:, :1]) * factor).astype(BF16)
            acc[h] = acc[h] * jnp.exp2((old - new) * factor) + jnp.dot(
                p, values, preferred_element_type=F32
            )
            mx[h] = new

    get_out.wait()
    for k in range(nhead):
        wsend[k] = wout_ref[:, k * cols:(k + 1) * cols]
    wo[hd] = wsend[hd]
    for k in range(nhead - 1):
        w_copy(k).start()
    for ch in range(2):
        sib_copy(0, 0, ch).wait_recv()
    attend(0)

    def arrive(s, last):
        for ch in (1, 0):
            for way in range(2):
                ring_copy(s, way, ch).wait_recv()
                if not last or way == ch:
                    ring_copy_next(s, way, ch, last).start()
                if ch == 0:
                    sib_copy(s, way, ch).start()
                else:
                    for k in range(nhead - 1):
                        f_copy(s, way, k).start()

    def projected(s, way):
        for k in range(nhead - 1):
            f_copy(s, way, k).wait_recv()
        made = []
        for i in (1, 2):
            total = jnp.zeros((half, width), F32)
            for k in range(nhead):
                w = wqkv_ref[i, k * cols:(k + 1) * cols, :]
                total = total + jnp.dot(fx[s, way, k], w, preferred_element_type=F32)
            made.append(total.astype(BF16))
        return made

    def digest(s):
        for way in range(2):
            made = projected(s, way)
            for i in range(2):
                kv[2 * s, way, part(1), i * width:(i + 1) * width] = made[i]
            sib_copy(s, way, 1).start()

    def ring_copy_next(s, way, ch, last):
        if last:
            return ring_copy(steps, way, ch)
        return ring_copy(s + 1, way, ch)

    def taken(s):
        for ch in range(2):
            for way in range(2):
                sib_copy(s, way, ch).wait_recv()

    def turn(i, carry):
        s = i + 2
        arrive(s, False)
        attend(2 * s - 1)
        digest(s)
        attend(2 * s)
        taken(s)
        return carry

    arrive(1, False)
    digest(1)
    attend(2)
    taken(1)
    lax.fori_loop(0, steps - 3, turn, 0)

    s = steps - 1
    arrive(s, True)
    for j in range(reach):
        b_copy(j).wait_recv()
        for k in range(nhead - 1):
            c_copy(j, k).start()
    attend(2 * s - 1)
    digest(s)
    attend(2 * s)
    get_live.wait()
    get_msg.wait()
    get_tiles.wait()
    for j in range(reach):
        for k in range(nhead - 1):
            c_copy(j, k).wait_recv()
    for r in range(row_blocks):
        total = [jnp.zeros((blk, cols), F32) for _ in range(nhead)]
        for t in range(slots):
            tile = tiles_ref[r, t]
            place = live_ref[r * slots + t:r * slots + t + 1, :]
            spread = jnp.concatenate(
                [tile * jnp.where(place == b, 1.0, 0.0).astype(BF16) for b in range(blocks)], axis=1
            )
            for k in range(nhead):
                total[k] = total[k] + jnp.dot(spread, table[k], preferred_element_type=F32)
        sent = jnp.zeros((blk, cols), F32)
        for k in range(nhead):
            sent = sent + jnp.dot(
                total[k].astype(BF16), wmsg_ref[k * cols:(k + 1) * cols, :], preferred_element_type=F32
            )
        msg[r * blk:(r + 1) * blk, :] = jnp.maximum(sent, 0.0) + table[hd, r * blk:(r + 1) * blk, :].astype(F32)
    ring_copy(steps, 1, 1).wait_recv()
    for k in range(nhead - 1):
        f_copy(steps, 1, k).start()
    ring_copy(steps, 0, 0).wait_recv()
    sib_copy(steps, 0, 0).start()
    taken(s)
    attend(2 * s + 1)
    made = projected(steps, 1)
    for i in range(2):
        kv[1, 0, part(1), i * width:(i + 1) * width] = made[i]
    sib_copy(steps, 0, 1).start()
    for ch in range(2):
        sib_copy(steps, 0, ch).wait_recv()
    attend(1)

    for t in range((heads + 1) // 2):
        made = jnp.zeros((rows, LANES), F32)
        for h in range(2 * t, min(2 * t + 2, heads)):
            a = acc[h]
            made = jnp.where(mine(h), a / pltpu.roll(a, DEPTH, 1), made)
        hg[hd, :, t * LANES:(t + 1) * LANES] = made.astype(BF16)
    for k in range(nhead - 1):
        h_copy(k).start()
    result = msg[...] + jnp.dot(hg[hd], wo[hd], preferred_element_type=F32)
    for k in range(nhead - 1):
        w_copy(k).wait_recv()
        h_copy(k).wait_recv()
    for k in range(1, nhead):
        other = (hd + k) % nhead
        result = result + jnp.dot(hg[other], wo[other], preferred_element_type=F32)
    out_ref[...] = result.astype(BF16)

    for k in range(nhead - 1):
        x_copy(k).wait_send()
        w_copy(k).wait_send()
        h_copy(k).wait_send()
        f_copy(steps, 1, k).wait_send()
    for j in range(reach):
        b_copy(j).wait_send()
        for k in range(nhead - 1):
            c_copy(j, k).wait_send()
    for ch in range(2):
        sib_copy(0, 0, ch).wait_send()
        sib_copy(steps, 0, ch).wait_send()
        ring_copy(steps, ch, ch).wait_send()
        for way in range(2):
            ring_copy(1, way, ch).wait_send()

    def sent_all(i, carry):
        for ch in range(2):
            for way in range(2):
                sib_copy(i + 1, way, ch).wait_send()
        for k in range(nhead - 1):
            for way in range(2):
                f_copy(i + 1, way, k).wait_send()
        return carry

    def sent_ring(i, carry):
        for ch in range(2):
            for way in range(2):
                ring_copy(i + 2, way, ch).wait_send()
        return carry

    lax.fori_loop(0, steps - 1, sent_all, 0)
    lax.fori_loop(0, steps - 2, sent_ring, 0)


def local(ndom, nhead, node_feats, tile_vals, tile_counts, tile_cols, send_rows, w_msg, w_qkv, w_out):
    rows, cols = node_feats.shape
    blk = tile_vals.shape[2]
    reach = send_rows.shape[1]
    heads = cols // DEPTH
    width = -(-cols // LANES) * LANES
    if width != cols:
        w_qkv = jnp.pad(w_qkv, ((0, 0), (0, 0), (0, width - cols)))
        w_out = jnp.pad(w_out, ((0, width - cols), (0, 0)))
    steps = ndom // 4
    dma = pltpu.SemaphoreType.DMA
    others = max(nhead - 1, 1)
    vmem = pl.BlockSpec(memory_space=pltpu.VMEM)
    slot = lax.broadcasted_iota(jnp.int32, tile_cols.shape, 1)
    live = jnp.where(slot < tile_counts[:, None], tile_cols, -1).reshape(-1, 1)
    live = jnp.broadcast_to(live, (live.shape[0], blk))
    return pl.pallas_call(
        functools.partial(body, ndom, nhead, 1.0 / math.sqrt(DEPTH)),
        out_shape=jax.ShapeDtypeStruct((rows, cols), BF16),
        in_specs=[pl.BlockSpec(memory_space=pltpu.HBM)] * 7,
        out_specs=vmem,
        scratch_shapes=[
            pltpu.VMEM(live.shape, jnp.int32),
            pltpu.VMEM(tile_vals.shape, BF16),
            pltpu.VMEM(send_rows.shape[1:], jnp.int32),
            pltpu.VMEM(w_msg.shape, BF16),
            pltpu.VMEM(w_qkv.shape, BF16),
            pltpu.VMEM(w_out.shape, BF16),
            dma((7,)),
            pltpu.VMEM((nhead, rows + reach * blk, cols), BF16),
            pltpu.VMEM((reach, blk, cols), BF16),
            pltpu.VMEM((nhead, width, cols), BF16),
            pltpu.VMEM((nhead, width, cols), BF16),
            pltpu.VMEM((2 * steps, 2, rows, 2 * width), BF16),
            pltpu.VMEM((heads, rows, LANES), BF16),
            pltpu.VMEM((heads, rows, LANES), F32),
            pltpu.VMEM((heads, rows, LANES), F32),
            pltpu.VMEM((nhead, rows, width), BF16),
            pltpu.VMEM((rows, cols), F32),
            dma((others,)), dma((others,)),
            dma((others,)), dma((others,)),
            dma((reach,)), dma((reach,)),
            dma((reach, others)), dma((reach, others)),
            dma((steps + 1, 2, 2)), dma((steps + 1, 2, 2)),
            dma((steps + 1, 2, 2)), dma((steps + 1, 2, 2)),
            dma((others,)), dma((others,)),
            dma((steps + 1, 2, others)), dma((steps + 1, 2, others)),
            pltpu.VMEM((steps + 1, 2, nhead, rows // 2, cols), BF16),
        ],
        compiler_params=pltpu.CompilerParams(
            collective_id=0, has_side_effects=True, vmem_limit_bytes=63 * 1024 * 1024
        ),
    )(live, node_feats, tile_vals, send_rows[0], w_msg, w_qkv, w_out)


def solution(mesh):
    placed = (
        P("dom", "head"),
        P("dom", None, None, None),
        P("dom"),
        P("dom", None),
        P("dom", None, None),
        P(None, "head"),
        P(None, None, "head"),
        P("head", None),
    )
    return jax.shard_map(
        functools.partial(local, mesh.shape["dom"], mesh.shape["head"]),
        mesh=mesh, in_specs=placed, out_specs=P("dom", "head"), check_vma=False,
    )
```

```python
import functools
import math

import jax
import jax.numpy as jnp
from jax import lax
from jax.experimental import pallas as pl
from jax.experimental.pallas import tpu as pltpu
from jax.sharding import PartitionSpec as P

DEPTH = 64
LANES = 128
MESH = pl.DeviceIdType.MESH
F32 = jnp.float32
BF16 = jnp.bfloat16


def offsets(count):
    reach = count // 2
    return [j - reach if j < reach else j - reach + 1 for j in range(count)]


def ring_next(chip, chips, step):
    depth = 4 if chips % 4 == 0 else 2
    width = chips // depth
    z, y = chip // width, chip % width
    if width == 1:
        return (chip + step + chips) % chips
    k = depth - 1 - z
    inner = width - 1
    odd = k % 2
    along = (1 - odd) * (y - 1) + odd * (width - 1 - y)
    first = 1 - jnp.minimum(y, 1)
    at = first * z + (1 - first) * (depth + k * inner + along)
    at = (at + step + chips) % chips
    far = 1 - jnp.minimum(jnp.maximum(at - (depth - 1), 0), 1)
    rest = jnp.maximum(at - depth, 0)
    k2 = rest // inner
    a2 = rest % inner
    odd2 = k2 % 2
    y2 = (1 - odd2) * (a2 + 1) + odd2 * (width - 1 - a2)
    z2 = depth - 1 - k2
    return far * (at * width) + (1 - far) * (z2 * width + y2)


def body(
    ndom, nhead, scale,
    live_in, x_ref, tiles_in, rows_in, wmsg_in, wqkv_in, wout_in,
    out_ref,
    live_ref, tiles_ref, rows_ref, wmsg_ref, wqkv_ref, wout_ref, in_sem,
    table, chosen, wsend, wo, kv, qs, mx, acc, hg, msg,
    x_send, x_recv, w_send, w_recv, b_send, b_recv, c_send, c_recv,
    r_send, r_recv, s_send, s_recv, h_send, h_recv,
):
    rows, cols = x_ref.shape
    width = qs.shape[2] * (kv.shape[3] // (2 * LANES))
    heads = qs.shape[0]
    half = rows // 2
    chips = ndom // 2
    steps = chips // 2
    blk = tiles_ref.shape[2]
    row_blocks, slots = tiles_ref.shape[0], tiles_ref.shape[1]
    reach = rows_ref.shape[0]
    blocks = row_blocks + reach
    me = lax.axis_index("dom")
    hd = lax.axis_index("head")
    chip, core = me // 2, me % 2
    right = (ring_next(chip, chips, 1) * 2 + core, hd)
    left = (ring_next(chip, chips, -1) * 2 + core, hd)
    sib = (chip * 2 + 1 - core, hd)
    near = [((me + o + ndom) % ndom, hd) for o in offsets(reach)]
    peers = [(me, (hd + k) % nhead) for k in range(1, nhead)]

    barrier = pltpu.get_barrier_semaphore()
    everyone = [right, left, sib] + near + peers
    for d in everyone:
        pl.semaphore_signal(barrier, inc=1, device_id=d, device_id_type=MESH)

    def fetch(i, src, dst):
        return pltpu.make_async_copy(src, dst, in_sem.at[i])

    get_x = fetch(0, x_ref, table.at[hd, pl.ds(0, rows)])
    get_qkv = fetch(1, wqkv_in, wqkv_ref)
    get_rows = fetch(2, rows_in, rows_ref)
    get_out = fetch(3, wout_in, wout_ref)
    get_live = fetch(4, live_in, live_ref)
    get_msg = fetch(5, wmsg_in, wmsg_ref)
    get_tiles = fetch(6, tiles_in, tiles_ref)
    for get in (get_x, get_qkv, get_rows, get_out, get_live, get_msg, get_tiles):
        get.start()
    pl.semaphore_wait(barrier, len(everyone))

    def copy(src, dst, ss, rs, to):
        return pltpu.make_async_remote_copy(
            src_ref=src, dst_ref=dst, send_sem=ss, recv_sem=rs, device_id=to, device_id_type=MESH
        )

    def x_copy(k):
        return copy(x_ref, table.at[hd, pl.ds(0, rows)], x_send.at[k], x_recv.at[k], peers[k])

    def w_copy(k):
        to = (hd + k + 1) % nhead
        return copy(wsend.at[to], wo.at[hd], w_send.at[k], w_recv.at[k], peers[k])

    def h_copy(k):
        return copy(hg.at[hd], hg.at[hd], h_send.at[k], h_recv.at[k], peers[k])

    def b_copy(j):
        dst = table.at[hd, pl.ds(rows + j * blk, blk)]
        return copy(chosen.at[j], dst, b_send.at[j], b_recv.at[j], near[j])

    def c_copy(j, k):
        both = table.at[hd, pl.ds(rows + j * blk, blk)]
        return copy(both, both, c_send.at[j, k], c_recv.at[j, k], peers[k])

    def part(ch):
        return pl.ds(ch * half, half)

    def ring_copy(s, way, ch):
        to = right if way == 0 else left
        if isinstance(s, int) and s == 1:
            src = kv.at[0, 0, part(ch)]
        else:
            src = kv.at[2 * s - 2, way, part(ch)]
        if isinstance(s, int) and s == steps:
            dst = kv.at[1, 0, part(ch)]
        else:
            dst = kv.at[2 * s, way, part(ch)]
        return copy(src, dst, r_send.at[s, way, ch], r_recv.at[s, way, ch], to)

    def sib_copy(s, way, ch):
        if isinstance(s, int) and s == 0:
            src, dst = kv.at[0, 0, part(ch)], kv.at[0, 1, part(ch)]
        elif isinstance(s, int) and s == steps:
            src, dst = kv.at[1, 0, part(ch)], kv.at[1, 1, part(ch)]
        else:
            src, dst = kv.at[2 * s, way, part(ch)], kv.at[2 * s + 1, way, part(ch)]
        return copy(src, dst, s_send.at[s, way, ch], s_recv.at[s, way, ch], sib)

    for k in range(nhead - 1):
        x_copy(k).start()

    def project(which, k, rs):
        w = wqkv_ref[which, pl.ds(pl.multiple_of(k * cols, cols), cols), :]
        x = table[k, rs, :]
        return jnp.dot(x, w, preferred_element_type=F32)

    def tiled(value, h):
        t = h // 2
        return value[:, t * LANES:(t + 1) * LANES]

    for h in range(heads):
        mx[h] = jnp.full((rows, LANES), -1e30, F32)
        acc[h] = jnp.zeros((rows, LANES), F32)

    get_x.wait()
    get_qkv.wait()
    whole = pl.ds(0, rows)
    begun = [project(i, hd, whole) for i in (1, 2)]
    for k in range(nhead - 1):
        x_copy(k).wait_recv()
    for k in range(1, nhead):
        other = (hd + k) % nhead
        begun = [b + project(i, other, whole) for b, i in zip(begun, (1, 2))]
    for ch in range(2):
        for i in range(2):
            kv[0, 0, part(ch), i * width:(i + 1) * width] = begun[i][ch * half:(ch + 1) * half].astype(BF16)
        for way in range(2):
            ring_copy(1, way, ch).start()
        sib_copy(0, 0, ch).start()

    lane = lax.broadcasted_iota(jnp.int32, (1, LANES), 1)

    def mine(h):
        return (lane // DEPTH) == (h % 2)

    query = project(0, hd, whole)
    for k in range(1, nhead):
        query = query + project(0, (hd + k) % nhead, whole)
    query = query.astype(BF16)
    for h in range(heads):
        tile = tiled(query, h)
        qs[h] = jnp.where(mine(h), tile, jnp.zeros_like(tile))

    get_rows.wait()
    line = lax.broadcasted_iota(jnp.int32, (rows, blk), 0)
    for j in range(reach):
        pick = jnp.where(line == rows_ref[j:j + 1, :], 1.0, 0.0).astype(BF16)
        got = lax.dot_general(
            pick, table[hd, pl.ds(0, rows), :], (((0,), (0,)), ((), ())), preferred_element_type=F32
        )
        chosen[j] = got.astype(BF16)
        b_copy(j).start()

    factor = scale * math.log2(math.e)

    def attend(at):
        for h in range(heads):
            t = h // 2
            keys = kv[at, :, :, t * LANES:(t + 1) * LANES].reshape(2 * rows, LANES)
            values = kv[at, :, :, width + t * LANES:width + (t + 1) * LANES].reshape(2 * rows, LANES)
            values = jnp.where(mine(h), values, jnp.ones_like(values))
            s = lax.dot_general(qs[h], keys, (((1,), (1,)), ((), ())), preferred_element_type=F32)
            old = mx[h]
            new = jnp.maximum(old, jnp.max(s, axis=1, keepdims=True))
            p = jnp.exp2((s - new[:, :1]) * factor).astype(BF16)
            acc[h] = acc[h] * jnp.exp2((old - new) * factor) + jnp.dot(
                p, values, preferred_element_type=F32
            )
            mx[h] = new

    get_out.wait()
    for k in range(nhead):
        wsend[k] = wout_ref[:, k * cols:(k + 1) * cols]
    wo[hd] = wsend[hd]
    for k in range(nhead - 1):
        w_copy(k).start()
    for ch in range(2):
        sib_copy(0, 0, ch).wait_recv()
    attend(0)

    def arrive(s, last):
        for ch in range(2):
            for way in range(2):
                ring_copy(s, way, ch).wait_recv()
                if not last or way == ch:
                    ring_copy_next(s, way, ch, last).start()
                sib_copy(s, way, ch).start()

    def ring_copy_next(s, way, ch, last):
        if last:
            return ring_copy(steps, way, ch)
        return ring_copy(s + 1, way, ch)

    def taken(s):
        for ch in range(2):
            for way in range(2):
                sib_copy(s, way, ch).wait_recv()

    def turn(i, carry):
        s = i + 1
        arrive(s, False)
        attend(2 * s)
        taken(s)
        attend(2 * s + 1)
        return carry

    lax.fori_loop(0, steps - 2, turn, 0)

    s = steps - 1
    arrive(s, True)
    for j in range(reach):
        b_copy(j).wait_recv()
        for k in range(nhead - 1):
            c_copy(j, k).start()
    attend(2 * s)
    for ch in range(2):
        ring_copy(steps, ch, ch).wait_recv()
        sib_copy(steps, 0, ch).start()
    taken(s)
    attend(2 * s + 1)
    get_live.wait()
    get_msg.wait()
    get_tiles.wait()
    for j in range(reach):
        for k in range(nhead - 1):
            c_copy(j, k).wait_recv()
    for r in range(row_blocks):
        total = [jnp.zeros((blk, cols), F32) for _ in range(nhead)]
        for t in range(slots):
            tile = tiles_ref[r, t]
            place = live_ref[r * slots + t:r * slots + t + 1, :]
            spread = jnp.concatenate(
                [tile * jnp.where(place == b, 1.0, 0.0).astype(BF16) for b in range(blocks)], axis=1
            )
            for k in range(nhead):
                total[k] = total[k] + jnp.dot(spread, table[k], preferred_element_type=F32)
        sent = jnp.zeros((blk, cols), F32)
        for k in range(nhead):
            sent = sent + jnp.dot(
                total[k].astype(BF16), wmsg_ref[k * cols:(k + 1) * cols, :], preferred_element_type=F32
            )
        msg[r * blk:(r + 1) * blk, :] = jnp.maximum(sent, 0.0) + table[hd, r * blk:(r + 1) * blk, :].astype(F32)
    for ch in range(2):
        sib_copy(steps, 0, ch).wait_recv()
    attend(1)

    for t in range((heads + 1) // 2):
        made = jnp.zeros((rows, LANES), F32)
        for h in range(2 * t, min(2 * t + 2, heads)):
            a = acc[h]
            made = jnp.where(mine(h), a / pltpu.roll(a, DEPTH, 1), made)
        hg[hd, :, t * LANES:(t + 1) * LANES] = made.astype(BF16)
    for k in range(nhead - 1):
        h_copy(k).start()
    result = msg[...] + jnp.dot(hg[hd], wo[hd], preferred_element_type=F32)
    for k in range(nhead - 1):
        w_copy(k).wait_recv()
        h_copy(k).wait_recv()
    for k in range(1, nhead):
        other = (hd + k) % nhead
        result = result + jnp.dot(hg[other], wo[other], preferred_element_type=F32)
    out_ref[...] = result.astype(BF16)

    for k in range(nhead - 1):
        x_copy(k).wait_send()
        w_copy(k).wait_send()
        h_copy(k).wait_send()
    for j in range(reach):
        b_copy(j).wait_send()
        for k in range(nhead - 1):
            c_copy(j, k).wait_send()
    for ch in range(2):
        sib_copy(0, 0, ch).wait_send()
        sib_copy(steps, 0, ch).wait_send()
        ring_copy(steps, ch, ch).wait_send()
        for way in range(2):
            ring_copy(1, way, ch).wait_send()

    def sent_all(i, carry):
        for ch in range(2):
            for way in range(2):
                sib_copy(i + 1, way, ch).wait_send()
        return carry

    def sent_ring(i, carry):
        for ch in range(2):
            for way in range(2):
                ring_copy(i + 2, way, ch).wait_send()
        return carry

    lax.fori_loop(0, steps - 1, sent_all, 0)
    lax.fori_loop(0, steps - 2, sent_ring, 0)


def local(ndom, nhead, node_feats, tile_vals, tile_counts, tile_cols, send_rows, w_msg, w_qkv, w_out):
    rows, cols = node_feats.shape
    blk = tile_vals.shape[2]
    reach = send_rows.shape[1]
    heads = cols // DEPTH
    width = -(-cols // LANES) * LANES
    if width != cols:
        w_qkv = jnp.pad(w_qkv, ((0, 0), (0, 0), (0, width - cols)))
        w_out = jnp.pad(w_out, ((0, width - cols), (0, 0)))
    steps = ndom // 4
    dma = pltpu.SemaphoreType.DMA
    others = max(nhead - 1, 1)
    vmem = pl.BlockSpec(memory_space=pltpu.VMEM)
    slot = lax.broadcasted_iota(jnp.int32, tile_cols.shape, 1)
    live = jnp.where(slot < tile_counts[:, None], tile_cols, -1).reshape(-1, 1)
    live = jnp.broadcast_to(live, (live.shape[0], blk))
    return pl.pallas_call(
        functools.partial(body, ndom, nhead, 1.0 / math.sqrt(DEPTH)),
        out_shape=jax.ShapeDtypeStruct((rows, cols), BF16),
        in_specs=[pl.BlockSpec(memory_space=pltpu.HBM)] * 7,
        out_specs=vmem,
        scratch_shapes=[
            pltpu.VMEM(live.shape, jnp.int32),
            pltpu.VMEM(tile_vals.shape, BF16),
            pltpu.VMEM(send_rows.shape[1:], jnp.int32),
            pltpu.VMEM(w_msg.shape, BF16),
            pltpu.VMEM(w_qkv.shape, BF16),
            pltpu.VMEM(w_out.shape, BF16),
            dma((7,)),
            pltpu.VMEM((nhead, rows + reach * blk, cols), BF16),
            pltpu.VMEM((reach, blk, cols), BF16),
            pltpu.VMEM((nhead, width, cols), BF16),
            pltpu.VMEM((nhead, width, cols), BF16),
            pltpu.VMEM((2 * steps, 2, rows, 2 * width), BF16),
            pltpu.VMEM((heads, rows, LANES), BF16),
            pltpu.VMEM((heads, rows, LANES), F32),
            pltpu.VMEM((heads, rows, LANES), F32),
            pltpu.VMEM((nhead, rows, width), BF16),
            pltpu.VMEM((rows, cols), F32),
            dma((others,)), dma((others,)),
            dma((others,)), dma((others,)),
            dma((reach,)), dma((reach,)),
            dma((reach, others)), dma((reach, others)),
            dma((steps + 1, 2, 2)), dma((steps + 1, 2, 2)),
            dma((steps + 1, 2, 2)), dma((steps + 1, 2, 2)),
            dma((others,)), dma((others,)),
        ],
        compiler_params=pltpu.CompilerParams(
            collective_id=0, has_side_effects=True, vmem_limit_bytes=63 * 1024 * 1024
        ),
    )(live, node_feats, tile_vals, send_rows[0], w_msg, w_qkv, w_out)


def solution(mesh):
    placed = (
        P("dom", "head"),
        P("dom", None, None, None),
        P("dom"),
        P("dom", None),
        P("dom", None, None),
        P(None, "head"),
        P(None, None, "head"),
        P("head", None),
    )
    return jax.shard_map(
        functools.partial(local, mesh.shape["dom"], mesh.shape["head"]),
        mesh=mesh, in_specs=placed, out_specs=P("dom", "head"), check_vma=False,
    )
```
